32 devices in a mesh: dp: 8 (over z, y), seq: 4 (over x, core).
Axes of the slice: x: 2, y: 2, z: 4, core: 2. Of those that a mesh axis runs over, the one named last changes fastest.
Arguments:
- signal: bfloat16 [8, 2048, 1536], P('dp', 'seq'), may hold values from -6 to 6
- norm_gain: bfloat16 [1536], replicated, may hold values from 0.5 to 1.5
- norm_bias: bfloat16 [1536], replicated, may hold values from -3 to 3
- expand_weight: bfloat16 [1536, 3072], P('dp'), may hold values from -0.15625 to 0.15625
- expand_bias: bfloat16 [3072], replicated, may hold values from -3 to 3
- depth_kernel: bfloat16 [31, 1536], replicated, may hold values from -1 to 1
- batch_scale: bfloat16 [1536], replicated, may hold values from 0.5 to 2
- batch_shift: bfloat16 [1536], replicated, may hold values from -3 to 3
- project_weight: bfloat16 [1536, 1536], P('dp'), may hold values from -0.15625 to 0.15625
- project_bias: bfloat16 [1536], replicated, may hold values from -3 to 3
Outputs:
- result: bfloat16 [8, 2048, 1536], P('dp', 'seq')
The draws below stay inside these ranges and needn't reach their ends.
All inputs are finite; a program needn't handle non-finite values.
Results may differ from the reference program's by a relative error of at most 0.0047.
Values may be sent and summed in bfloat16 or wider, within the bound.
No kernel may reach another device: no remote copies, remote signals or barrier semaphores. Data moves between devices by JAX's collectives and lax.ppermute only.
A program may use at most 64 MiB of HBM per device.

```python
import math
import jax
import jax.numpy as jnp
from jax import lax

D = 1536
K = 31
HALF = 15
FRAMES = 2048
RECS = 8


def block_scale(rng, dims, shards, low, largest):
    def one(position, parts):
        steps = jax.random.uniform(jax.random.fold_in(jax.random.fold_in(rng, 6), position), (parts,), jnp.float32, low / len(shards), largest / len(shards))
        return jnp.repeat(jnp.exp(steps), dims[position] // parts).reshape((-1,) + (1,) * (len(dims) - position - 1))

    level = one(*shards[0])
    for cut in shards[1:]:
        level = level * one(*cut)
    return level


def gaussian(rng, shape, scale, bound, split=(), kind=jnp.bfloat16):
    factor_of = block_scale(rng, shape, split, -0.22, 0.18) if split else 1.0
    values = jax.random.normal(rng, shape, jnp.float32) * scale * factor_of
    return jnp.minimum(jnp.maximum(values, -bound), bound).astype(kind)


def setup_inputs(seed: int = 0) -> dict:
    seeds = jax.random.split(jax.random.key(seed), 11)
    signal = gaussian(seeds[0], (RECS, FRAMES, D), 1.0, 6.0, ((0, 8), (1, 4)))
    norm_gain = jnp.clip(1.0 + 0.1 * jax.random.normal(seeds[1], (D,), jnp.float32), 0.5, 1.5).astype(jnp.bfloat16)
    norm_bias = gaussian(seeds[2], (D,), 0.5, 3.0)
    expand_weight = gaussian(seeds[3], (D, 2 * D), D ** -0.5, 0.15625, ((0, 8),))
    expand_bias = gaussian(seeds[4], (2 * D,), 0.5, 3.0)
    depth_kernel = gaussian(seeds[5], (K, D), K ** -0.5, 1.0)
    batch_scale = jnp.clip(jnp.exp(jax.random.uniform(seeds[6], (D,), jnp.float32, math.log(0.5), math.log(2.0))), 0.5, 2.0).astype(jnp.bfloat16)
    batch_shift = gaussian(seeds[7], (D,), 0.5, 3.0)
    project_weight = gaussian(seeds[8], (D, D), D ** -0.5, 0.15625, ((0, 8),))
    project_bias = gaussian(seeds[9], (D,), 0.5, 3.0)
    return dict(signal=signal, norm_gain=norm_gain, norm_bias=norm_bias, expand_weight=expand_weight, expand_bias=expand_bias, depth_kernel=depth_kernel, batch_scale=batch_scale, batch_shift=batch_shift, project_weight=project_weight, project_bias=project_bias)


def one_recording(frames_in, norm_gain, norm_bias, expand_weight, expand_bias, depth_kernel, batch_scale, batch_shift, project_weight, project_bias):
    values = frames_in.astype(jnp.float32)
    average = lax.optimization_barrier(jnp.mean(values, axis=-1, keepdims=True))
    centred = values - average
    spread = lax.optimization_barrier(jnp.mean(centred * centred, axis=-1, keepdims=True))
    normed = (centred * lax.rsqrt(spread + 1e-05) * norm_gain.astype(jnp.float32) + norm_bias.astype(jnp.float32)).astype(jnp.bfloat16)
    hidden = jnp.dot(normed, expand_weight, preferred_element_type=jnp.float32) + expand_bias.astype(jnp.float32)
    width = frames_in.shape[1]
    gated = (hidden[:, :width] * jax.nn.sigmoid(hidden[:, width:])).astype(jnp.bfloat16)
    padded = jnp.pad(gated.astype(jnp.float32), ((HALF, HALF), (0, 0)))
    kernel = depth_kernel.astype(jnp.float32)
    length = frames_in.shape[0]
    depth = jnp.zeros((length, width), jnp.float32)
    for tap in range(K):
        depth = depth + kernel[tap][None, :] * padded[tap:tap + length]
    scaled = depth * batch_scale.astype(jnp.float32) + batch_shift.astype(jnp.float32)
    activated = (scaled * jax.nn.sigmoid(scaled)).astype(jnp.bfloat16)
    mixed = jnp.dot(activated, project_weight, preferred_element_type=jnp.float32)
    return (values + mixed + project_bias.astype(jnp.float32)).astype(jnp.bfloat16)

def reference(signal, norm_gain, norm_bias, expand_weight, expand_bias, depth_kernel, batch_scale, batch_shift, project_weight, project_bias):

    def per_record(frames_in):
        return one_recording(frames_in, norm_gain, norm_bias, expand_weight, expand_bias, depth_kernel, batch_scale, batch_shift, project_weight, project_bias)
    return lax.map(per_record, signal)
```

```python
import functools

import jax
import jax.numpy as jnp
from jax import lax
from jax.experimental import pallas as pl
from jax.experimental.pallas import tpu as pltpu
from jax.sharding import PartitionSpec as P

LANES = 128
VMEM_LIMIT = 48 * 1024 * 1024
ANY = pl.BlockSpec(memory_space=pl.ANY)
VMEM = pl.BlockSpec(memory_space=pltpu.VMEM)


def params(**kw):
    return pltpu.CompilerParams(vmem_limit_bytes=VMEM_LIMIT, **kw)


def sigmoid(x):
    return 0.5 + 0.5 * jnp.tanh(0.5 * x)


GAIN, NBIAS, VBIAS, GBIAS, BSCALE, BSHIFT, PBIAS, TAPS = 0, 1, 2, 3, 4, 5, 6, 8


def norm_body(signal, packed, out):
    values = signal[...].astype(jnp.float32)
    average = jnp.mean(values, axis=-1, keepdims=True)
    centred = values - average
    spread = jnp.mean(centred * centred, axis=-1, keepdims=True)
    out[...] = (
        centred * lax.rsqrt(spread + 1e-05) * packed[GAIN : GAIN + 1, :]
        + packed[NBIAS : NBIAS + 1, :]
    ).astype(jnp.bfloat16)


def norm(signal, packed):
    frames, width = signal.shape
    tile = 128
    return pl.pallas_call(
        norm_body,
        grid=(frames // tile,),
        in_specs=[
            pl.BlockSpec((tile, width), lambda i: (i, 0)),
            pl.BlockSpec((8, width), lambda i: (0, 0)),
        ],
        out_specs=pl.BlockSpec((tile, width), lambda i: (i, 0)),
        out_shape=jax.ShapeDtypeStruct((frames, width), jnp.bfloat16),
        compiler_params=params(),
        cost_estimate=pl.CostEstimate(
            flops=10 * frames * width, bytes_accessed=4 * frames * width, transcendentals=frames
        ),
        name="layer_norm",
    )(signal, packed)


def conv_body(offset, share, taps, packed, first, second, third, fourth, *refs):
    normed, outs = refs[:4], refs[4:8]
    weight, frames_in, gated, sems = refs[8:]
    seq, dp = lax.axis_index("seq"), lax.axis_index("dp")
    rows = first.shape[0] // 2
    channels = outs[0].shape[1]
    length = normed[0].shape[0]
    total = 4 * length
    half = (taps - 1) // 2

    copies = []
    for which, pair in enumerate((first, second, third, fourth)):
        for k in range(2):
            owner = dp ^ ((which % 2) * 4 + k * 2) ^ (which // 2)
            copies.append(
                pltpu.make_async_copy(
                    pair.at[pl.ds(k * rows, rows)],
                    weight.at[pl.ds(pl.multiple_of(owner * rows, 16), rows)],
                    sems.at[len(copies)],
                )
            )
    blocks = []
    for k in range(4):
        start = pl.multiple_of((seq ^ k) * length, length)
        blocks.append(
            pltpu.make_async_copy(
                normed[k], frames_in.at[pl.ds(start, length)], sems.at[len(copies) + k]
            )
        )
    for copy in copies + blocks:
        copy.start()

    base = seq * share + offset
    lanes = [pl.ds(pl.multiple_of(base + LANES * b, LANES), LANES) for b in range(channels // LANES)]
    value_bias = jnp.concatenate([packed[VBIAS : VBIAS + 1, at] for at in lanes], axis=1)
    gate_bias = jnp.concatenate([packed[GBIAS : GBIAS + 1, at] for at in lanes], axis=1)
    edge = jnp.zeros((16, LANES), jnp.float32)
    for b in range(len(lanes)):
        gated[b, 0:16, :] = edge
        gated[b, 16 + total : 32 + total, :] = edge
    for copy in copies:
        copy.wait()

    tile = 256
    for k in range(4):
        blocks[k].wait()

        def expand(i, _, k=k):
            start = pl.multiple_of((seq ^ k) * length + i * tile, tile)
            hidden = jnp.dot(
                frames_in[pl.ds(start, tile), :], weight[...], preferred_element_type=jnp.float32
            )
            result = (hidden[:, :channels] + value_bias) * sigmoid(hidden[:, channels:] + gate_bias)
            for b in range(len(lanes)):
                gated[b, pl.ds(16 + start, tile), :] = result[:, b * LANES : (b + 1) * LANES]
            return 0

        lax.fori_loop(0, length // tile, expand, 0)

    step = 64
    for b, at in enumerate(lanes):
        kernel = [packed[TAPS + t : TAPS + t + 1, at] for t in range(taps)]
        scale, shift = packed[BSCALE : BSCALE + 1, at], packed[BSHIFT : BSHIFT + 1, at]
        for k in range(4):

            def depthwise(i, _, k=k, b=b, kernel=kernel, scale=scale, shift=shift):
                start = pl.multiple_of((seq ^ k) * length + i * step, step)
                depth = jnp.zeros((step, LANES), jnp.float32)
                for t in range(taps):
                    depth = depth + kernel[t] * gated[b, pl.ds(start + (16 - half + t), step), :]
                scaled = depth * scale + shift
                outs[k][pl.ds(pl.multiple_of(i * step, step), step), b * LANES : (b + 1) * LANES] = (
                    scaled * sigmoid(scaled)
                ).astype(jnp.bfloat16)
                return 0

            lax.fori_loop(0, length // step, depthwise, 0)


def conv(offset, channels, share, taps, packed, pairs, normed):
    length, width = normed[0].shape
    flops = 2 * 4 * length * width * 2 * channels
    return pl.pallas_call(
        functools.partial(conv_body, offset, share, taps),
        in_specs=[VMEM] + [ANY] * 8,
        out_specs=[VMEM] * 4,
        out_shape=[jax.ShapeDtypeStruct((length, channels), jnp.bfloat16)] * 4,
        scratch_shapes=[
            pltpu.VMEM((width, 2 * channels), jnp.bfloat16),
            pltpu.VMEM((4 * length, width), jnp.bfloat16),
            pltpu.VMEM((channels // LANES, 4 * length + 32, LANES), jnp.float32),
            pltpu.SemaphoreType.DMA((12,)),
        ],
        compiler_params=params(),
        cost_estimate=pl.CostEstimate(
            flops=4 * flops, bytes_accessed=8 * length * width, transcendentals=0
        ),
        name="expand_and_depthwise",
    )(packed, *pairs, *normed)


def project_body(chunks, share, signal, packed, *refs):
    count = 4 * len(chunks)
    acts, pairs, out = refs[:count], refs[count : count + 8], refs[count + 8]
    weight, left, sems = refs[count + 9 :]
    seq, dp = lax.axis_index("seq"), lax.axis_index("dp")
    rows = pairs[0].shape[0] // 2
    cols = pairs[0].shape[1]
    copies = []

    def add(source, target):
        copies.append(pltpu.make_async_copy(source, target, sems.at[len(copies)]))

    for side in range(2):
        at = pl.ds(pl.multiple_of(((seq & 1) ^ side) * cols, LANES), cols)
        for which in range(4):
            for k in range(2):
                owner = dp ^ ((which % 2) * 4 + k * 2) ^ (which // 2)
                add(
                    pairs[4 * side + which].at[pl.ds(k * rows, rows)],
                    weight.at[pl.ds(pl.multiple_of(owner * rows, 16), rows), at],
                )
    for j, (offset, channels) in enumerate(chunks):
        for k in range(4):
            at = pl.ds(pl.multiple_of((seq ^ k) * share + offset, LANES), channels)
            add(acts[4 * j + k], left.at[:, at])
    for copy in copies:
        copy.start()
    for copy in copies:
        copy.wait()
    tile = 128

    def one(i, _):
        at = pl.ds(pl.multiple_of(i * tile, tile), tile)
        mixed = jnp.dot(left[at, :], weight[...], preferred_element_type=jnp.float32)
        out[at, :] = (
            signal[at, :].astype(jnp.float32) + mixed + packed[PBIAS : PBIAS + 1, :]
        ).astype(jnp.bfloat16)
        return 0

    lax.fori_loop(0, out.shape[0] // tile, one, 0)


def project(chunks, share, signal, packed, acts, pairs):
    length, width = signal.shape
    return pl.pallas_call(
        functools.partial(project_body, chunks, share),
        in_specs=[VMEM, VMEM] + [ANY] * (len(acts) + len(pairs)),
        out_specs=VMEM,
        out_shape=jax.ShapeDtypeStruct((length, width), jnp.bfloat16),
        scratch_shapes=[
            pltpu.VMEM((width, width), jnp.bfloat16),
            pltpu.VMEM((length, width), jnp.bfloat16),
            pltpu.SemaphoreType.DMA((len(acts) + 16,)),
        ],
        compiler_params=params(),
        cost_estimate=pl.CostEstimate(
            flops=2 * length * width * width, bytes_accessed=2 * width * width, transcendentals=0
        ),
        name="project_and_residual",
    )(signal, packed, *acts, *pairs)


def across(array, axis, bits):
    count = lax.axis_size(axis)
    return lax.ppermute(array, axis, [(i, i ^ bits) for i in range(count)])


def spread(own):
    near = across(own, "dp", 2)
    far = across(own, "dp", 4)
    diagonal = across(own, "dp", 6)
    first = jnp.concatenate([own, near], axis=0)
    second = jnp.concatenate([far, diagonal], axis=0)
    return [first, second, across(first, "dp", 1), across(second, "dp", 1)]


def on_the_plane(
    signal, norm_gain, norm_bias, expand_weight, expand_bias, depth_kernel,
    batch_scale, batch_shift, project_weight, project_bias,
):
    width = signal.shape[2]
    taps = depth_kernel.shape[0]
    seq = lax.axis_index("seq")
    share = width // 4
    chunks = ((0, 256), (256, 128))
    pad = jnp.zeros((1, width), jnp.bfloat16)
    packed = jnp.concatenate(
        [
            norm_gain[None], norm_bias[None], expand_bias.reshape(2, width), batch_scale[None],
            batch_shift[None], project_bias[None], pad, depth_kernel, pad,
        ],
        axis=0,
    ).astype(jnp.float32)

    weights = []
    for offset, channels in chunks:
        value = lax.dynamic_slice_in_dim(expand_weight, seq * share + offset, channels, 1)
        gate = lax.dynamic_slice_in_dim(expand_weight, width + seq * share + offset, channels, 1)
        weights.append(spread(jnp.concatenate([value, gate], axis=1)))

    normed = norm(signal[0], packed)
    beside = across(normed, "seq", 1)
    facing = across(normed, "seq", 2)
    normed = [normed, beside, facing, across(facing, "seq", 1)]

    half = width // 2
    mine = spread(lax.dynamic_slice_in_dim(project_weight, (seq & 1) * half, half, 1))
    pairs = mine + [across(pair, "seq", 1) for pair in mine]

    acts = []
    for (offset, channels), pieces in zip(chunks, weights):
        parts = conv(offset, channels, share, taps, packed, pieces, normed)
        acts += [parts[0]] + [across(parts[k], "seq", k) for k in range(1, 4)]
    return project(chunks, share, signal[0], packed, acts, pairs)[None]


def extended(block, sides, width):
    for axis, dim in sides:
        count = lax.axis_size(axis)
        forward = [(i, i + 1) for i in range(count - 1)]
        backward = [(target, source) for source, target in forward]
        low = lax.ppermute(
            lax.slice_in_dim(block, block.shape[dim] - width, None, axis=dim), axis, forward
        )
        high = lax.ppermute(lax.slice_in_dim(block, 0, width, axis=dim), axis, backward)
        block = jnp.concatenate([low, block, high], axis=dim)
    return block


def fold_rows(left_side, blocks):
    return jnp.dot(left_side, blocks, preferred_element_type=jnp.float32)


def gathered(
    signal, norm_gain, norm_bias, expand_weight, expand_bias, depth_kernel,
    batch_scale, batch_shift, project_weight, project_bias,
):
    length = signal.shape[1]
    width = signal.shape[2]
    values = signal[0].astype(jnp.float32)
    average = jnp.mean(values, axis=-1, keepdims=True)
    centred = values - average
    spread = jnp.mean(centred * centred, axis=-1, keepdims=True)
    normed = (
        centred * lax.rsqrt(spread + 1e-05) * norm_gain.astype(jnp.float32)
        + norm_bias.astype(jnp.float32)
    ).astype(jnp.bfloat16)
    hidden = fold_rows(normed, lax.all_gather(expand_weight, "dp", axis=0, tiled=True))
    hidden = hidden + expand_bias.astype(jnp.float32)
    gated = (hidden[:, :width] * jax.nn.sigmoid(hidden[:, width:])).astype(jnp.bfloat16)
    halo_width = (depth_kernel.shape[0] - 1) // 2
    padded = extended(gated[None], (("seq", 1),), halo_width)[0].astype(jnp.float32)
    kernel = depth_kernel.astype(jnp.float32)
    depth = jnp.zeros((length, width), jnp.float32)
    for tap in range(depth_kernel.shape[0]):
        depth = depth + kernel[tap][None, :] * padded[tap : tap + length]
    scaled = depth * batch_scale.astype(jnp.float32) + batch_shift.astype(jnp.float32)
    activated = (scaled * jax.nn.sigmoid(scaled)).astype(jnp.bfloat16)
    mixed = fold_rows(activated, lax.all_gather(project_weight, "dp", axis=0, tiled=True))
    outcome = values + mixed + project_bias.astype(jnp.float32)
    return outcome.astype(jnp.bfloat16)[None]


def solution(mesh):
    local = on_the_plane if (mesh.shape["dp"], mesh.shape["seq"]) == (8, 4) else gathered
    in_specs = (
        P("dp", "seq", None),
        P(),
        P(),
        P("dp", None),
        P(),
        P(),
        P(),
        P(),
        P("dp", None),
        P(),
    )
    out_specs = P("dp", "seq", None)
    return jax.shard_map(local, mesh=mesh, in_specs=in_specs, out_specs=out_specs, check_vma=False)
```

```python
import functools

import jax
import jax.numpy as jnp
from jax import lax
from jax.experimental import pallas as pl
from jax.experimental.pallas import tpu as pltpu
from jax.sharding import PartitionSpec as P

LANES = 128
LARGE = 60 * 1024 * 1024
CONV = 24 * 1024 * 1024
ANY = pl.BlockSpec(memory_space=pl.ANY)
VMEM = pl.BlockSpec(memory_space=pltpu.VMEM)


def params(limit=32 * 1024 * 1024):
    return pltpu.CompilerParams(vmem_limit_bytes=limit)


def sigmoid(x):
    return 0.5 + 0.5 * jnp.tanh(0.5 * x)


GAIN, NBIAS, VBIAS, GBIAS, BSCALE, BSHIFT, PBIAS = range(7)
EDGE = 16
PIECES = (208, 416)
FREE = pl.CostEstimate(flops=0, bytes_accessed=0, transcendentals=0)


def cut_body(cuts, signal, expand, project, first, second, *refs):
    pieces, sems = refs[:-1], refs[-1]
    seq = lax.axis_index("seq")
    share = first.shape[1] // 2
    half = second.shape[1]
    width = expand.shape[1] // 2
    copies = []

    def add(source, target):
        copies.append(pltpu.make_async_copy(source, target, sems.at[len(copies)]))

    for side in range(2):
        at = pl.ds(pl.multiple_of(side * width + seq * share, LANES), share)
        add(expand.at[:, at], first.at[:, side * share : (side + 1) * share])
    add(project.at[:, pl.ds(pl.multiple_of((seq & 1) * half, LANES), half)], second)
    for (start, stop), piece in zip(cuts, pieces):
        add(signal.at[start:stop], piece)
    for copy in copies:
        copy.start()
    for copy in copies:
        copy.wait()


def cut(cuts, signal, expand, project, parts):
    rows, width = project.shape
    share = width // parts
    shapes = [(rows, 2 * share), (rows, width // 2)] + [(b - a, width) for a, b in cuts]
    return pl.pallas_call(
        functools.partial(cut_body, cuts),
        in_specs=[ANY] * 3,
        out_specs=[VMEM] * len(shapes),
        out_shape=[jax.ShapeDtypeStruct(shape, expand.dtype) for shape in shapes],
        scratch_shapes=[pltpu.SemaphoreType.DMA((len(cuts) + 3,))],
        compiler_params=params(LARGE),
        cost_estimate=FREE,
        name="cut",
    )(signal, expand, project)


def norm_body(packed, *refs):
    pieces, out = refs[:-1], refs[-1]
    base = 0
    for piece in pieces:
        tile = next(t for t in (128, 104, 96, 16) if piece.shape[0] % t == 0)

        def one(i, _, piece=piece, base=base, tile=tile):
            at = pl.multiple_of(i * tile, tile)
            values = piece[pl.ds(at, tile), :].astype(jnp.float32)
            average = jnp.mean(values, axis=-1, keepdims=True)
            centred = values - average
            spread = jnp.mean(centred * centred, axis=-1, keepdims=True)
            out[pl.ds(base + at, tile), :] = (
                centred * lax.rsqrt(spread + 1e-05) * packed[GAIN : GAIN + 1, :]
                + packed[NBIAS : NBIAS + 1, :]
            ).astype(jnp.bfloat16)
            return 0

        lax.fori_loop(0, piece.shape[0] // tile, one, 0)
        base += piece.shape[0]


def norm(packed, *pieces):
    width = packed.shape[1]
    return pl.pallas_call(
        norm_body,
        in_specs=[VMEM] * (1 + len(pieces)),
        out_specs=VMEM,
        out_shape=jax.ShapeDtypeStruct((sum(p.shape[0] for p in pieces), width), jnp.bfloat16),
        compiler_params=params(),
        cost_estimate=FREE,
        name="layer_norm",
    )(packed, *pieces)


def gather_body(places, *refs):
    pieces, out, sems = refs[: len(places)], refs[-2], refs[-1]
    dp = lax.axis_index("dp")
    rows = pieces[0].shape[0]
    copies = []
    for piece, (bits, first) in zip(pieces, places):
        at = pl.multiple_of((dp ^ bits) * rows + first, 16)
        copies.append(
            pltpu.make_async_copy(piece, out.at[pl.ds(at, piece.shape[0])], sems.at[len(copies)])
        )
    for copy in copies:
        copy.start()
    for copy in copies:
        copy.wait()


def gather(places, pieces):
    rows = sum(piece.shape[0] for piece in pieces)
    return pl.pallas_call(
        functools.partial(gather_body, places),
        in_specs=[ANY] * len(pieces),
        out_specs=VMEM,
        out_shape=jax.ShapeDtypeStruct((rows, pieces[0].shape[1]), pieces[0].dtype),
        scratch_shapes=[pltpu.SemaphoreType.DMA((len(pieces),))],
        compiler_params=params(),
        cost_estimate=FREE,
        name="gather_shards",
    )(*pieces)


def conv_body(across_x, across_core, packed, kernel, weight, block, sibling, outer, out, frames, gated, taps):
    seq = lax.axis_index("seq")
    chip, odd = (seq >> 1) ^ across_x, (seq & 1) ^ across_core
    length, channels = out.shape
    count = kernel.shape[0]
    half = (count - 1) // 2
    lanes = [
        pl.ds(pl.multiple_of(seq * channels + LANES * b, LANES), LANES)
        for b in range(channels // LANES)
    ]
    for b, at in enumerate(lanes):
        taps[b, 0:count, :] = kernel[:, at].astype(jnp.float32)
    frames[EDGE : EDGE + length, :] = block[...]
    for edges, first in ((sibling, odd), (outer, 1 - odd)):
        source = pl.ds(pl.multiple_of(first * (edges.shape[0] - EDGE), EDGE), EDGE)
        frames[pl.ds(pl.multiple_of((1 - first) * (EDGE + length), EDGE), EDGE), :] = edges[source, :]
    starts = jnp.logical_and(chip == 0, odd == 0)
    ends = jnp.logical_and(chip == 1, odd == 1)

    def expand(b):
        columns = jnp.concatenate(
            [
                weight[:, b * LANES : (b + 1) * LANES],
                weight[:, channels + b * LANES : channels + (b + 1) * LANES],
            ],
            axis=1,
        )
        hidden = jnp.dot(frames[...], columns, preferred_element_type=jnp.float32)
        value = hidden[:, :LANES] + packed[VBIAS : VBIAS + 1, lanes[b]]
        gate = hidden[:, LANES:] + packed[GBIAS : GBIAS + 1, lanes[b]]
        result = value * sigmoid(gate)
        gated[b, 0:EDGE, :] = jnp.where(starts, 0.0, result[0:EDGE, :])
        gated[b, EDGE : EDGE + length, :] = result[EDGE : EDGE + length, :]
        gated[b, EDGE + length :, :] = jnp.where(ends, 0.0, result[EDGE + length :, :])

    step = 64

    def depthwise(b):
        at = lanes[b]
        scale, shift = packed[BSCALE : BSCALE + 1, at], packed[BSHIFT : BSHIFT + 1, at]
        for start in range(0, length, step):
            depth = jnp.zeros((step, LANES), jnp.float32)
            for t in range(count):
                first = start + EDGE - half + t
                depth = depth + taps[b, t : t + 1, :] * gated[b, first : first + step, :]
            scaled = depth * scale + shift
            out[start : start + step, b * LANES : (b + 1) * LANES] = (
                scaled * sigmoid(scaled)
            ).astype(jnp.bfloat16)

    for b in range(len(lanes)):
        expand(b)
        if b:
            depthwise(b - 1)
    depthwise(len(lanes) - 1)


def conv(across_x, across_core, packed, kernel, weight, block, sibling, outer):
    length, width = block.shape
    channels = weight.shape[1] // 2
    extent = length + 2 * EDGE
    return pl.pallas_call(
        functools.partial(conv_body, across_x, across_core),
        in_specs=[VMEM] * 6,
        out_specs=VMEM,
        out_shape=jax.ShapeDtypeStruct((length, channels), jnp.bfloat16),
        scratch_shapes=[
            pltpu.VMEM((extent, width), jnp.bfloat16),
            pltpu.VMEM((channels // LANES, extent, LANES), jnp.float32),
            pltpu.VMEM((channels // LANES, kernel.shape[0] + 1, LANES), jnp.float32),
        ],
        compiler_params=params(CONV),
        cost_estimate=FREE,
        name="expand_and_depthwise",
    )(packed, kernel, weight, block, sibling, outer)


def project_body(places, packed, signal, whole, *refs):
    count = 2 * len(places)
    pieces, acts, out = refs[:count], refs[count : count + 4], refs[count + 4]
    weight, left, frames, result, sems = refs[count + 5 :]
    seq, dp = lax.axis_index("seq"), lax.axis_index("dp")
    share = acts[0].shape[1]
    rows, cols = whole.shape[0], pieces[0].shape[1]
    length = out.shape[0]
    tile = 256
    copies = []

    def add(source, target):
        copies.append(pltpu.make_async_copy(source, target, sems.at[len(copies)]))
        copies[-1].start()

    ats = [pl.ds(pl.multiple_of(((seq & 1) ^ side) * cols, LANES), cols) for side in range(2)]
    for side in range(2):
        sources = [(whole.at[:, ats[side]], 0, 0)]
        sources += [
            (piece, *place) for piece, place in zip(pieces[side * len(places) :], places)
        ]
        for source, bits, first in sources:
            at = pl.ds(pl.multiple_of((dp ^ bits) * rows + first, 16), source.shape[0])
            add(source, weight.at[side, at])
        if side == 0:
            for k in range(4):
                at = pl.ds(pl.multiple_of((seq ^ k) * share, LANES), share)
                add(acts[k], left.at[:, at])
            add(signal, frames)
    split = len(places) + 6
    parts = []
    for side, ready in enumerate((copies[:split], copies[split:])):
        for copy in ready:
            copy.wait()
        for start in range(0, length, tile):
            mixed = jnp.dot(
                left[start : start + tile, :], weight[side], preferred_element_type=jnp.float32
            )
            mixed = mixed + packed[PBIAS : PBIAS + 1, ats[side]]
            mixed = mixed + frames[start : start + tile, ats[side]].astype(jnp.float32)
            result[side, start : start + tile, :] = mixed.astype(jnp.bfloat16)
            part = pltpu.make_async_copy(
                result.at[side, start : start + tile],
                out.at[start : start + tile, ats[side]],
                sems.at[len(copies) + len(parts)],
            )
            part.start()
            parts.append(part)
    for part in parts:
        part.wait()


def project(packed, signal, whole, places, mine, other, acts):
    length, width = signal.shape
    return pl.pallas_call(
        functools.partial(project_body, places),
        in_specs=[VMEM] + [ANY] * (2 + 2 * len(places) + 4),
        out_specs=ANY,
        out_shape=jax.ShapeDtypeStruct((length, width), jnp.bfloat16),
        scratch_shapes=[
            pltpu.VMEM((2, width, width // 2), jnp.bfloat16),
            pltpu.VMEM((length, width), jnp.bfloat16),
            pltpu.VMEM((length, width), jnp.bfloat16),
            pltpu.VMEM((2, length, width // 2), jnp.bfloat16),
            pltpu.SemaphoreType.DMA((2 * len(places) + 7 + 2 * (length // 256),)),
        ],
        compiler_params=params(),
        cost_estimate=FREE,
        name="project_and_residual",
    )(packed, signal, whole, *mine, *other, *acts)


def across(array, axis, bits):
    count = lax.axis_size(axis)
    return lax.ppermute(array, axis, [(i, i ^ bits) for i in range(count)])


def after(array, *others):
    return lax.optimization_barrier((array, *others))[0]


def on_the_plane(
    signal, norm_gain, norm_bias, expand_weight, expand_bias, depth_kernel,
    batch_scale, batch_shift, project_weight, project_bias,
):
    width = signal.shape[2]
    own = signal[0]
    length = own.shape[0]
    marks = [0, PIECES[0], PIECES[1], length]
    cuts = list(zip(marks[:-1], marks[1:]))
    e_own, p_own, *pieces = cut(cuts, own, expand_weight, project_weight, 4)
    fold = p_own.shape[0] // 2

    facing = [across(pieces[0], "seq", 2)]
    e_far, e_near = across(e_own, "dp", 6), across(e_own, "dp", 2)
    ey_own, py_own = across(e_own, "dp", 1), across(p_own, "dp", 1)
    done = (facing[0], e_far, e_near, ey_own, py_own)

    facing.append(across(after(pieces[1], *done), "seq", 2))
    e_middle = across(after(e_own, *done), "dp", 4)
    p_near = across(after(p_own, *done), "dp", 2)
    ey_near, ey_far = across(after(e_near, *done), "dp", 1), across(after(e_far, *done), "dp", 1)
    packed = (
        jnp.concatenate(
            [after(norm_gain, *done), norm_bias, expand_bias, batch_scale, batch_shift, project_bias]
        )
        .reshape(7, width)
        .astype(jnp.float32)
    )
    normed = norm(packed, own)
    edges = jnp.concatenate([normed[:EDGE], normed[-EDGE:]], axis=0)
    done = (facing[1], e_middle, p_near, ey_near, ey_far)

    facing.append(across(after(pieces[2], *done), "seq", 2))
    ey_middle = across(after(e_middle, *done), "dp", 1)
    p_far = [across(after(p_own[:fold], *done), "dp", 6)]
    edges = across(after(edges, *done), "seq", 3)
    beside = across(after(normed, *done), "seq", 1)
    e_shards = [e_own, e_near, e_middle, e_far, ey_own, ey_near, ey_middle, ey_far]
    done = (facing[2], ey_middle, p_far[0], edges, beside)

    normed_facing = norm(packed, after(facing[0], *done), *facing[1:])
    diagonal = across(normed_facing, "seq", 1)
    p_far.append(across(after(p_own[fold:], *done), "dp", 6))
    py_near = across(after(p_near, *done), "dp", 1)
    py_far = [across(p_far[0], "dp", 1)]
    weight = gather([(2 * (k % 4) + k // 4, 0) for k in range(8)], e_shards)
    run = functools.partial(conv, packed=packed, kernel=depth_kernel, weight=weight)
    part_facing = run(1, 0, block=normed_facing, sibling=edges, outer=beside)
    done = (part_facing, diagonal, p_far[1])

    act_facing = across(part_facing, "seq", 2)
    p_middle = across(after(p_own, *done), "dp", 4)
    py_far.append(across(after(p_far[1], *done), "dp", 1))
    part_diagonal = run(1, 1, block=after(diagonal, *done), sibling=normed_facing, outer=normed)
    done = (part_diagonal, py_near, py_far[0])

    act_diagonal = across(part_diagonal, "seq", 3)
    swap = lambda array: across(after(array, *done), "seq", 1)
    p_mine = [p_near, p_far[0], py_own, py_near]
    p_other = [swap(piece) for piece in p_mine]
    part_beside = run(0, 1, block=after(beside, *done), sibling=normed, outer=normed_facing)
    done = (part_beside, p_middle, py_far[1], act_facing)

    act_beside = across(part_beside, "seq", 1)
    py_middle = across(after(p_middle, *done), "dp", 1)
    late = [p_far[1], py_far[0], py_far[1], p_middle]
    p_mine += late
    p_other += [swap(piece) for piece in late]
    part_own = run(0, 0, block=after(normed, *done), sibling=beside, outer=diagonal)
    p_mine.append(py_middle)
    p_other.append(across(after(py_middle, part_own), "seq", 1))
    places = [(2, 0), (6, 0), (1, 0), (3, 0), (6, fold), (7, 0), (7, fold), (4, 0), (5, 0)]
    acts = [part_own, act_beside, act_facing, act_diagonal]
    return project(packed, own, project_weight, places, p_mine, p_other, acts)[None]


def extended(block, sides, width):
    for axis, dim in sides:
        count = lax.axis_size(axis)
        forward = [(i, i + 1) for i in range(count - 1)]
        backward = [(target, source) for source, target in forward]
        low = lax.ppermute(
            lax.slice_in_dim(block, block.shape[dim] - width, None, axis=dim), axis, forward
        )
        high = lax.ppermute(lax.slice_in_dim(block, 0, width, axis=dim), axis, backward)
        block = jnp.concatenate([low, block, high], axis=dim)
    return block


def fold_rows(left_side, blocks):
    return jnp.dot(left_side, blocks, preferred_element_type=jnp.float32)


def gathered(
    signal, norm_gain, norm_bias, expand_weight, expand_bias, depth_kernel,
    batch_scale, batch_shift, project_weight, project_bias,
):
    length = signal.shape[1]
    width = signal.shape[2]
    values = signal[0].astype(jnp.float32)
    average = jnp.mean(values, axis=-1, keepdims=True)
    centred = values - average
    spread = jnp.mean(centred * centred, axis=-1, keepdims=True)
    normed = (
        centred * lax.rsqrt(spread + 1e-05) * norm_gain.astype(jnp.float32)
        + norm_bias.astype(jnp.float32)
    ).astype(jnp.bfloat16)
    hidden = fold_rows(normed, lax.all_gather(expand_weight, "dp", axis=0, tiled=True))
    hidden = hidden + expand_bias.astype(jnp.float32)
    gated = (hidden[:, :width] * jax.nn.sigmoid(hidden[:, width:])).astype(jnp.bfloat16)
    halo_width = (depth_kernel.shape[0] - 1) // 2
    padded = extended(gated[None], (("seq", 1),), halo_width)[0].astype(jnp.float32)
    kernel = depth_kernel.astype(jnp.float32)
    depth = jnp.zeros((length, width), jnp.float32)
    for tap in range(depth_kernel.shape[0]):
        depth = depth + kernel[tap][None, :] * padded[tap : tap + length]
    scaled = depth * batch_scale.astype(jnp.float32) + batch_shift.astype(jnp.float32)
    activated = (scaled * jax.nn.sigmoid(scaled)).astype(jnp.bfloat16)
    mixed = fold_rows(activated, lax.all_gather(project_weight, "dp", axis=0, tiled=True))
    outcome = values + mixed + project_bias.astype(jnp.float32)
    return outcome.astype(jnp.bfloat16)[None]


def solution(mesh):
    local = on_the_plane if (mesh.shape["dp"], mesh.shape["seq"]) == (8, 4) else gathered
    in_specs = (
        P("dp", "seq", None),
        P(),
        P(),
        P("dp", None),
        P(),
        P(),
        P(),
        P(),
        P("dp", None),
        P(),
    )
    out_specs = P("dp", "seq", None)
    return jax.shard_map(local, mesh=mesh, in_specs=in_specs, out_specs=out_specs, check_vma=False)
```

```python
import functools

import jax
import jax.numpy as jnp
from jax import lax
from jax.experimental import pallas as pl
from jax.experimental.pallas import tpu as pltpu
from jax.sharding import PartitionSpec as P

LANES = 128
LARGE = 60 * 1024 * 1024
CONV = 24 * 1024 * 1024
ANY = pl.BlockSpec(memory_space=pl.ANY)
VMEM = pl.BlockSpec(memory_space=pltpu.VMEM)


def params(limit=32 * 1024 * 1024):
    return pltpu.CompilerParams(vmem_limit_bytes=limit)


def sigmoid(x):
    return 0.5 + 0.5 * jnp.tanh(0.5 * x)


GAIN, NBIAS, VBIAS, GBIAS, BSCALE, BSHIFT, PBIAS = range(7)
EDGE = 16
FREE = pl.CostEstimate(flops=0, bytes_accessed=0, transcendentals=0)


def cut_body(expand, project, first, second, both, sems):
    seq = lax.axis_index("seq")
    share = first.shape[1] // 2
    half = second.shape[1]
    width = expand.shape[1] // 2
    copies = []

    def add(source, target):
        copies.append(pltpu.make_async_copy(source, target, sems.at[len(copies)]))

    for side in range(2):
        at = pl.ds(pl.multiple_of(side * width + seq * share, LANES), share)
        for target in (first, both):
            add(expand.at[:, at], target.at[:, side * share : (side + 1) * share])
    at = pl.ds(pl.multiple_of((seq & 1) * half, LANES), half)
    add(project.at[:, at], second)
    add(project.at[:, at], both.at[:, 2 * share :])
    for copy in copies:
        copy.start()
    for copy in copies:
        copy.wait()


def cut(expand, project, parts):
    rows, width = project.shape
    shapes = [(rows, 2 * width // parts), (rows, width // 2)]
    shapes.append((rows, shapes[0][1] + shapes[1][1]))
    return pl.pallas_call(
        cut_body,
        in_specs=[ANY] * 2,
        out_specs=[VMEM] * len(shapes),
        out_shape=[jax.ShapeDtypeStruct(shape, expand.dtype) for shape in shapes],
        scratch_shapes=[pltpu.SemaphoreType.DMA((6,))],
        compiler_params=params(LARGE),
        cost_estimate=FREE,
        name="cut_weights",
    )(expand, project)


def norm_body(packed, *refs):
    pieces, out = refs[:-1], refs[-1]
    base = 0
    for piece in pieces:
        tile = next(t for t in (128, 64, 16) if piece.shape[0] % t == 0)

        def one(i, _, piece=piece, base=base, tile=tile):
            at = pl.multiple_of(i * tile, tile)
            values = piece[pl.ds(at, tile), :].astype(jnp.float32)
            average = jnp.mean(values, axis=-1, keepdims=True)
            centred = values - average
            spread = jnp.mean(centred * centred, axis=-1, keepdims=True)
            out[pl.ds(base + at, tile), :] = (
                centred * lax.rsqrt(spread + 1e-05) * packed[GAIN : GAIN + 1, :]
                + packed[NBIAS : NBIAS + 1, :]
            ).astype(jnp.bfloat16)
            return 0

        lax.fori_loop(0, piece.shape[0] // tile, one, 0)
        base += piece.shape[0]


def norm(packed, *pieces):
    width = packed.shape[1]
    return pl.pallas_call(
        norm_body,
        in_specs=[VMEM] * (1 + len(pieces)),
        out_specs=VMEM,
        out_shape=jax.ShapeDtypeStruct((sum(p.shape[0] for p in pieces), width), jnp.bfloat16),
        compiler_params=params(),
        cost_estimate=FREE,
        name="layer_norm",
    )(packed, *pieces)


def gather_body(places, *refs):
    pieces, out, sems = refs[: len(places)], refs[-2], refs[-1]
    dp = lax.axis_index("dp")
    rows, cols = pieces[0].shape[0], out.shape[1]
    copies = []
    for i, (piece, (bits, first)) in enumerate(zip(pieces, places)):
        at = i * rows if bits is None else pl.multiple_of((dp ^ bits) * rows, 16)
        copies.append(
            pltpu.make_async_copy(
                piece.at[:, first : first + cols], out.at[pl.ds(at, rows)], sems.at[i]
            )
        )
    for copy in copies:
        copy.start()
    for copy in copies:
        copy.wait()


def gather(places, pieces):
    rows, cols = pieces[0].shape
    return pl.pallas_call(
        functools.partial(gather_body, places),
        in_specs=[ANY] * len(pieces),
        out_specs=VMEM,
        out_shape=jax.ShapeDtypeStruct((rows * len(pieces), cols), pieces[0].dtype),
        scratch_shapes=[pltpu.SemaphoreType.DMA((len(pieces),))],
        compiler_params=params(),
        cost_estimate=FREE,
        name="gather_shards",
    )(*pieces)


def conv_body(across_x, across_core, packed, kernel, weight, block, sibling, outer, *refs):
    seq = lax.axis_index("seq")
    chip, odd = (seq >> 1) ^ across_x, (seq & 1) ^ across_core
    outs, (frames, gated, taps) = refs[:-3], refs[-3:]
    part, channels = outs[0].shape
    length = part * len(outs)
    count = kernel.shape[0]
    half = (count - 1) // 2
    lanes = [
        pl.ds(pl.multiple_of(seq * channels + LANES * b, LANES), LANES)
        for b in range(channels // LANES)
    ]
    for b, at in enumerate(lanes):
        taps[b, 0:count, :] = kernel[:, at].astype(jnp.float32)
    frames[EDGE : EDGE + length, :] = block[...]
    for edges, first in ((sibling, odd), (outer, 1 - odd)):
        source = pl.ds(pl.multiple_of(first * (edges.shape[0] - EDGE), EDGE), EDGE)
        frames[pl.ds(pl.multiple_of((1 - first) * (EDGE + length), EDGE), EDGE), :] = edges[source, :]
    starts = jnp.logical_and(chip == 0, odd == 0)
    ends = jnp.logical_and(chip == 1, odd == 1)

    def expand(b):
        columns = jnp.concatenate(
            [
                weight[:, b * LANES : (b + 1) * LANES],
                weight[:, channels + b * LANES : channels + (b + 1) * LANES],
            ],
            axis=1,
        )
        hidden = jnp.dot(frames[...], columns, preferred_element_type=jnp.float32)
        value = hidden[:, :LANES] + packed[VBIAS : VBIAS + 1, lanes[b]]
        gate = hidden[:, LANES:] + packed[GBIAS : GBIAS + 1, lanes[b]]
        result = value * sigmoid(gate)
        gated[b, 0:EDGE, :] = jnp.where(starts, 0.0, result[0:EDGE, :])
        gated[b, EDGE : EDGE + length, :] = result[EDGE : EDGE + length, :]
        gated[b, EDGE + length :, :] = jnp.where(ends, 0.0, result[EDGE + length :, :])

    step = 64

    def depthwise(b):
        at = lanes[b]
        scale, shift = packed[BSCALE : BSCALE + 1, at], packed[BSHIFT : BSHIFT + 1, at]
        for start in range(0, length, step):
            depth = jnp.zeros((step, LANES), jnp.float32)
            for t in range(count):
                first = start + EDGE - half + t
                depth = depth + taps[b, t : t + 1, :] * gated[b, first : first + step, :]
            scaled = depth * scale + shift
            at = start % part
            outs[start // part][at : at + step, b * LANES : (b + 1) * LANES] = (
                scaled * sigmoid(scaled)
            ).astype(jnp.bfloat16)

    for b in range(len(lanes)):
        expand(b)
        if b:
            depthwise(b - 1)
    depthwise(len(lanes) - 1)


def conv(across_x, across_core, parts, packed, kernel, weight, block, sibling, outer):
    length, width = block.shape
    channels = weight.shape[1] // 2
    extent = length + 2 * EDGE
    return pl.pallas_call(
        functools.partial(conv_body, across_x, across_core),
        in_specs=[VMEM] * 6,
        out_specs=[VMEM] * parts,
        out_shape=[jax.ShapeDtypeStruct((length // parts, channels), jnp.bfloat16)] * parts,
        scratch_shapes=[
            pltpu.VMEM((extent, width), jnp.bfloat16),
            pltpu.VMEM((channels // LANES, extent, LANES), jnp.float32),
            pltpu.VMEM((channels // LANES, kernel.shape[0] + 1, LANES), jnp.float32),
        ],
        compiler_params=params(CONV),
        cost_estimate=FREE,
        name="expand_and_depthwise",
    )(packed, kernel, weight, block, sibling, outer)


def project_body(places, spots, packed, signal, whole, *refs):
    count = 1 + max(which for side in places for which, _, _ in side)
    pieces, acts, out = refs[:count], refs[count:-6], refs[-6]
    weight, left, frames, result, sems = refs[-5:]
    seq, dp = lax.axis_index("seq"), lax.axis_index("dp")
    share = acts[0].shape[1]
    rows, cols = whole.shape[0], weight.shape[2]
    length = out.shape[0]
    tile = 256
    copies = []

    def add(source, target):
        copies.append(pltpu.make_async_copy(source, target, sems.at[len(copies)]))
        copies[-1].start()

    ats = [pl.ds(pl.multiple_of(((seq & 1) ^ side) * cols, LANES), cols) for side in range(2)]
    split = []
    for side in range(2):
        add(whole.at[:, ats[side]], weight.at[side, pl.ds(pl.multiple_of(dp * rows, 16), rows)])
        for which, first, bits in places[side]:
            add(
                pieces[which].at[first : first + rows],
                weight.at[side, pl.ds(pl.multiple_of((dp ^ bits) * rows, 16), rows)],
            )
        if side == 0:
            for act, (k, first) in zip(acts, spots):
                at = pl.ds(pl.multiple_of((seq ^ k) * share, LANES), share)
                add(act, left.at[first : first + act.shape[0], at])
            add(signal, frames)
            split = len(copies)
    parts = []
    for side, ready in enumerate((copies[:split], copies[split:])):
        for copy in ready:
            copy.wait()
        for start in range(0, length, tile):
            mixed = jnp.dot(
                left[start : start + tile, :], weight[side], preferred_element_type=jnp.float32
            )
            mixed = mixed + packed[PBIAS : PBIAS + 1, ats[side]]
            mixed = mixed + frames[start : start + tile, ats[side]].astype(jnp.float32)
            result[side, start : start + tile, :] = mixed.astype(jnp.bfloat16)
            part = pltpu.make_async_copy(
                result.at[side, start : start + tile],
                out.at[start : start + tile, ats[side]],
                sems.at[len(copies) + len(parts)],
            )
            part.start()
            parts.append(part)
    for part in parts:
        part.wait()


def project(packed, signal, whole, places, pieces, spots, acts):
    length, width = signal.shape
    return pl.pallas_call(
        functools.partial(project_body, places, spots),
        in_specs=[VMEM] + [ANY] * (2 + len(pieces) + len(acts)),
        out_specs=ANY,
        out_shape=jax.ShapeDtypeStruct((length, width), jnp.bfloat16),
        scratch_shapes=[
            pltpu.VMEM((2, width, width // 2), jnp.bfloat16),
            pltpu.VMEM((length, width), jnp.bfloat16),
            pltpu.VMEM((length, width), jnp.bfloat16),
            pltpu.VMEM((2, length, width // 2), jnp.bfloat16),
            pltpu.SemaphoreType.DMA((sum(map(len, places)) + 3 + len(acts) + 2 * (length // 256),)),
        ],
        compiler_params=params(),
        cost_estimate=FREE,
        name="project_and_residual",
    )(packed, signal, whole, *pieces, *acts)


def across(array, axis, bits):
    count = lax.axis_size(axis)
    return lax.ppermute(array, axis, [(i, i ^ bits) for i in range(count)])


def after(array, *others):
    return lax.optimization_barrier((array, *others))[0]


def on_the_plane(
    signal, norm_gain, norm_bias, expand_weight, expand_bias, depth_kernel,
    batch_scale, batch_shift, project_weight, project_bias,
):
    width = signal.shape[2]
    own = signal[0]
    e_own, p_own, both = cut(expand_weight, project_weight, 4)
    beside = across(own, "seq", 1)
    facing = across(after(own, e_own), "seq", 2)
    e_far, e_near = across(e_own, "dp", 6), across(e_own, "dp", 2)
    y_own = across(both, "dp", 1)
    done = (e_far, e_near, y_own)

    e_middle = across(after(e_own, *done), "dp", 4)
    p_near = across(after(p_own, *done), "dp", 2)
    ey_near, ey_far = across(after(e_near, *done), "dp", 1), across(after(e_far, *done), "dp", 1)
    packed = (
        jnp.concatenate(
            [after(norm_gain, *done), norm_bias, expand_bias, batch_scale, batch_shift, project_bias]
        )
        .reshape(7, width)
        .astype(jnp.float32)
    )
    normed = norm(packed, own)
    beside = norm(packed, beside)
    edges = jnp.concatenate([normed[:EDGE], normed[-EDGE:]], axis=0)
    done = (facing, e_middle, p_near, ey_near, ey_far, beside, edges)

    ey_middle = across(after(e_middle, *done), "dp", 1)
    p_far = across(after(p_own, *done), "dp", 6)
    edges = across(after(edges, *done), "seq", 3)
    py_near = across(after(p_near, *done), "dp", 1)
    normed_facing = norm(packed, after(facing, *done))
    diagonal = across(normed_facing, "seq", 1)
    e_shards = [e_own, e_near, e_middle, e_far, y_own, ey_near, ey_middle, ey_far]
    weight = gather([(2 * (k % 4) + k // 4, 0) for k in range(8)], e_shards)
    done = (ey_middle, edges, diagonal)

    run = functools.partial(conv, packed=packed, kernel=depth_kernel, weight=weight)
    part_facing = run(
        1, 0, 2, block=after(normed_facing, *done), sibling=edges, outer=beside
    )
    act_facing = [across(part, "seq", 2) for part in part_facing]
    p_middle = across(after(p_own, ey_middle, edges), "dp", 4)
    py_far = across(after(p_far, part_facing[0]), "dp", 1)
    done = (part_facing[0], p_far, py_near)

    [part_diagonal] = run(
        1, 1, 1, block=after(diagonal, *done), sibling=normed_facing, outer=normed
    )
    act_diagonal = across(part_diagonal, "seq", 3)
    [part_beside] = run(
        0, 1, 1, block=after(beside, part_diagonal), sibling=normed, outer=normed_facing
    )
    act_beside = across(part_beside, "seq", 1)
    [part_own] = run(
        0, 0, 1, block=after(normed, part_beside, py_far, *act_facing), sibling=beside, outer=diagonal
    )
    py_middle = across(after(p_middle, part_own), "dp", 1)
    columns = e_own.shape[1]
    early = gather([(None, 0), (None, columns)], [after(p_near, ey_middle), y_own])
    early_other = across(early, "seq", 1)
    late = [py_near, p_far, py_far, p_middle, py_middle]
    done = (part_own, act_diagonal, early_other)
    swapped = [across(after(shard, *done), "seq", 1) for shard in late]
    rows = e_own.shape[0]
    places = [
        [((1 + len(late)) * side, rows * k, bits) for k, bits in enumerate([2, 1])]
        + [((1 + len(late)) * side + 1 + k, 0, bits) for k, bits in enumerate([3, 6, 7, 4, 5])]
        for side in range(2)
    ]
    acts = [part_own, act_beside, act_diagonal, *act_facing]
    tall = own.shape[0] // len(act_facing)
    spots = [(0, 0), (1, 0), (3, 0)] + [(2, tall * k) for k in range(len(act_facing))]
    return project(packed, own, project_weight, places, [early, *late, early_other, *swapped], spots, acts)[None]


def extended(block, sides, width):
    for axis, dim in sides:
        count = lax.axis_size(axis)
        forward = [(i, i + 1) for i in range(count - 1)]
        backward = [(target, source) for source, target in forward]
        low = lax.ppermute(
            lax.slice_in_dim(block, block.shape[dim] - width, None, axis=dim), axis, forward
        )
        high = lax.ppermute(lax.slice_in_dim(block, 0, width, axis=dim), axis, backward)
        block = jnp.concatenate([low, block, high], axis=dim)
    return block


def fold_rows(left_side, blocks):
    return jnp.dot(left_side, blocks, preferred_element_type=jnp.float32)


def gathered(
    signal, norm_gain, norm_bias, expand_weight, expand_bias, depth_kernel,
    batch_scale, batch_shift, project_weight, project_bias,
):
    length = signal.shape[1]
    width = signal.shape[2]
    values = signal[0].astype(jnp.float32)
    average = jnp.mean(values, axis=-1, keepdims=True)
    centred = values - average
    spread = jnp.mean(centred * centred, axis=-1, keepdims=True)
    normed = (
        centred * lax.rsqrt(spread + 1e-05) * norm_gain.astype(jnp.float32)
        + norm_bias.astype(jnp.float32)
    ).astype(jnp.bfloat16)
    hidden = fold_rows(normed, lax.all_gather(expand_weight, "dp", axis=0, tiled=True))
    hidden = hidden + expand_bias.astype(jnp.float32)
    gated = (hidden[:, :width] * jax.nn.sigmoid(hidden[:, width:])).astype(jnp.bfloat16)
    halo_width = (depth_kernel.shape[0] - 1) // 2
    padded = extended(gated[None], (("seq", 1),), halo_width)[0].astype(jnp.float32)
    kernel = depth_kernel.astype(jnp.float32)
    depth = jnp.zeros((length, width), jnp.float32)
    for tap in range(depth_kernel.shape[0]):
        depth = depth + kernel[tap][None, :] * padded[tap : tap + length]
    scaled = depth * batch_scale.astype(jnp.float32) + batch_shift.astype(jnp.float32)
    activated = (scaled * jax.nn.sigmoid(scaled)).astype(jnp.bfloat16)
    mixed = fold_rows(activated, lax.all_gather(project_weight, "dp", axis=0, tiled=True))
    outcome = values + mixed + project_bias.astype(jnp.float32)
    return outcome.astype(jnp.bfloat16)[None]


def solution(mesh):
    local = on_the_plane if (mesh.shape["dp"], mesh.shape["seq"]) == (8, 4) else gathered
    in_specs = (
        P("dp", "seq", None),
        P(),
        P(),
        P("dp", None),
        P(),
        P(),
        P(),
        P(),
        P("dp", None),
        P(),
    )
    out_specs = P("dp", "seq", None)
    return jax.shard_map(local, mesh=mesh, in_specs=in_specs, out_specs=out_specs, check_vma=False)
```

```python
import functools

import jax
import jax.numpy as jnp
from jax import lax
from jax.experimental import pallas as pl
from jax.experimental.pallas import tpu as pltpu
from jax.sharding import PartitionSpec as P

LANES = 128
LARGE = 60 * 1024 * 1024
CONV = 24 * 1024 * 1024
ANY = pl.BlockSpec(memory_space=pl.ANY)
VMEM = pl.BlockSpec(memory_space=pltpu.VMEM)


def params(limit=32 * 1024 * 1024):
    return pltpu.CompilerParams(vmem_limit_bytes=limit)


def sigmoid(x):
    return 0.5 + 0.5 * jnp.tanh(0.5 * x)


GAIN, NBIAS, VBIAS, GBIAS, BSCALE, BSHIFT, PBIAS = range(7)
EDGE = 16
FREE = pl.CostEstimate(flops=0, bytes_accessed=0, transcendentals=0)


def cut_body(expand, project, first, second, both, sems):
    seq = lax.axis_index("seq")
    share = first.shape[1] // 2
    half = second.shape[1]
    width = expand.shape[1] // 2
    copies = []

    def add(source, target):
        copies.append(pltpu.make_async_copy(source, target, sems.at[len(copies)]))

    for side in range(2):
        at = pl.ds(pl.multiple_of(side * width + seq * share, LANES), share)
        for target in (first, both):
            add(expand.at[:, at], target.at[:, side * share : (side + 1) * share])
    at = pl.ds(pl.multiple_of((seq & 1) * half, LANES), half)
    add(project.at[:, at], second)
    add(project.at[:, at], both.at[:, 2 * share :])
    for copy in copies:
        copy.start()
    for copy in copies:
        copy.wait()


def cut(expand, project, parts):
    rows, width = project.shape
    shapes = [(rows, 2 * width // parts), (rows, width // 2)]
    shapes.append((rows, shapes[0][1] + shapes[1][1]))
    return pl.pallas_call(
        cut_body,
        in_specs=[ANY] * 2,
        out_specs=[VMEM] * len(shapes),
        out_shape=[jax.ShapeDtypeStruct(shape, expand.dtype) for shape in shapes],
        scratch_shapes=[pltpu.SemaphoreType.DMA((6,))],
        compiler_params=params(LARGE),
        cost_estimate=FREE,
        name="cut_weights",
    )(expand, project)


def norm_body(packed, *refs):
    pieces, out = refs[:-1], refs[-1]
    base = 0
    for piece in pieces:
        tile = next(t for t in (128, 64, 16) if piece.shape[0] % t == 0)

        def one(i, _, piece=piece, base=base, tile=tile):
            at = pl.multiple_of(i * tile, tile)
            values = piece[pl.ds(at, tile), :].astype(jnp.float32)
            average = jnp.mean(values, axis=-1, keepdims=True)
            centred = values - average
            spread = jnp.mean(centred * centred, axis=-1, keepdims=True)
            out[pl.ds(base + at, tile), :] = (
                centred * lax.rsqrt(spread + 1e-05) * packed[GAIN : GAIN + 1, :]
                + packed[NBIAS : NBIAS + 1, :]
            ).astype(jnp.bfloat16)
            return 0

        lax.fori_loop(0, piece.shape[0] // tile, one, 0)
        base += piece.shape[0]


def norm(packed, *pieces):
    width = packed.shape[1]
    return pl.pallas_call(
        norm_body,
        in_specs=[VMEM] * (1 + len(pieces)),
        out_specs=VMEM,
        out_shape=jax.ShapeDtypeStruct((sum(p.shape[0] for p in pieces), width), jnp.bfloat16),
        compiler_params=params(),
        cost_estimate=FREE,
        name="layer_norm",
    )(packed, *pieces)


def gather_body(places, *refs):
    pieces, out, sems = refs[: len(places)], refs[-2], refs[-1]
    dp = lax.axis_index("dp")
    rows, cols = pieces[0].shape[0], out.shape[1]
    copies = []
    for i, (piece, (bits, first)) in enumerate(zip(pieces, places)):
        at = i * rows if bits is None else pl.multiple_of((dp ^ bits) * rows, 16)
        copies.append(
            pltpu.make_async_copy(
                piece.at[:, first : first + cols], out.at[pl.ds(at, rows)], sems.at[i]
            )
        )
    for copy in copies:
        copy.start()
    for copy in copies:
        copy.wait()


def gather(places, pieces):
    rows, cols = pieces[0].shape
    return pl.pallas_call(
        functools.partial(gather_body, places),
        in_specs=[ANY] * len(pieces),
        out_specs=VMEM,
        out_shape=jax.ShapeDtypeStruct((rows * len(pieces), cols), pieces[0].dtype),
        scratch_shapes=[pltpu.SemaphoreType.DMA((len(pieces),))],
        compiler_params=params(),
        cost_estimate=FREE,
        name="gather_shards",
    )(*pieces)


def conv_body(across_x, across_core, packed, kernel, weight, block, sibling, outer, *refs):
    seq = lax.axis_index("seq")
    chip, odd = (seq >> 1) ^ across_x, (seq & 1) ^ across_core
    outs, (frames, gated, taps) = refs[:-3], refs[-3:]
    part, channels = outs[0].shape
    length = part * len(outs)
    count = kernel.shape[0]
    half = (count - 1) // 2
    lanes = [
        pl.ds(pl.multiple_of(seq * channels + LANES * b, LANES), LANES)
        for b in range(channels // LANES)
    ]
    for b, at in enumerate(lanes):
        taps[b, 0:count, :] = kernel[:, at].astype(jnp.float32)
    frames[EDGE : EDGE + length, :] = block[...]
    for edges, first in ((sibling, odd), (outer, 1 - odd)):
        source = pl.ds(pl.multiple_of(first * (edges.shape[0] - EDGE), EDGE), EDGE)
        frames[pl.ds(pl.multiple_of((1 - first) * (EDGE + length), EDGE), EDGE), :] = edges[source, :]
    starts = jnp.logical_and(chip == 0, odd == 0)
    ends = jnp.logical_and(chip == 1, odd == 1)

    def expand(b):
        columns = jnp.concatenate(
            [
                weight[:, b * LANES : (b + 1) * LANES],
                weight[:, channels + b * LANES : channels + (b + 1) * LANES],
            ],
            axis=1,
        )
        hidden = jnp.dot(frames[...], columns, preferred_element_type=jnp.float32)
        value = hidden[:, :LANES] + packed[VBIAS : VBIAS + 1, lanes[b]]
        gate = hidden[:, LANES:] + packed[GBIAS : GBIAS + 1, lanes[b]]
        result = value * sigmoid(gate)
        gated[b, 0:EDGE, :] = jnp.where(starts, 0.0, result[0:EDGE, :])
        gated[b, EDGE : EDGE + length, :] = result[EDGE : EDGE + length, :]
        gated[b, EDGE + length :, :] = jnp.where(ends, 0.0, result[EDGE + length :, :])

    step = 64

    def depthwise(b):
        at = lanes[b]
        scale, shift = packed[BSCALE : BSCALE + 1, at], packed[BSHIFT : BSHIFT + 1, at]
        for start in range(0, length, step):
            depth = jnp.zeros((step, LANES), jnp.float32)
            for t in range(count):
                first = start + EDGE - half + t
                depth = depth + taps[b, t : t + 1, :] * gated[b, first : first + step, :]
            scaled = depth * scale + shift
            at = start % part
            outs[start // part][at : at + step, b * LANES : (b + 1) * LANES] = (
                scaled * sigmoid(scaled)
            ).astype(jnp.bfloat16)

    for b in range(len(lanes)):
        expand(b)
        if b:
            depthwise(b - 1)
    depthwise(len(lanes) - 1)


def conv(across_x, across_core, parts, packed, kernel, weight, block, sibling, outer):
    length, width = block.shape
    channels = weight.shape[1] // 2
    extent = length + 2 * EDGE
    return pl.pallas_call(
        functools.partial(conv_body, across_x, across_core),
        in_specs=[VMEM] * 6,
        out_specs=[VMEM] * parts,
        out_shape=[jax.ShapeDtypeStruct((length // parts, channels), jnp.bfloat16)] * parts,
        scratch_shapes=[
            pltpu.VMEM((extent, width), jnp.bfloat16),
            pltpu.VMEM((channels // LANES, extent, LANES), jnp.float32),
            pltpu.VMEM((channels // LANES, kernel.shape[0] + 1, LANES), jnp.float32),
        ],
        compiler_params=params(CONV),
        cost_estimate=FREE,
        name="expand_and_depthwise",
    )(packed, kernel, weight, block, sibling, outer)


def project_body(places, spots, packed, signal, whole, *refs):
    count = 1 + max(which for side in places for which, _, _ in side)
    pieces, acts, out = refs[:count], refs[count:-6], refs[-6]
    weight, left, frames, result, sems = refs[-5:]
    seq, dp = lax.axis_index("seq"), lax.axis_index("dp")
    share = acts[0].shape[1]
    rows, cols = whole.shape[0], weight.shape[2]
    length = out.shape[0]
    tile = 256
    copies = []

    def add(source, target):
        copies.append(pltpu.make_async_copy(source, target, sems.at[len(copies)]))
        copies[-1].start()

    ats = [pl.ds(pl.multiple_of(((seq & 1) ^ side) * cols, LANES), cols) for side in range(2)]
    split = []
    for side in range(2):
        add(whole.at[:, ats[side]], weight.at[side, pl.ds(pl.multiple_of(dp * rows, 16), rows)])
        for which, first, bits in places[side]:
            add(
                pieces[which].at[first : first + rows],
                weight.at[side, pl.ds(pl.multiple_of((dp ^ bits) * rows, 16), rows)],
            )
        if side == 0:
            for act, (k, first) in zip(acts, spots):
                at = pl.ds(pl.multiple_of((seq ^ k) * share, LANES), share)
                add(act, left.at[first : first + act.shape[0], at])
            add(signal, frames)
            split = len(copies)
    parts = []
    for side, ready in enumerate((copies[:split], copies[split:])):
        for copy in ready:
            copy.wait()
        for start in range(0, length, tile):
            mixed = jnp.dot(
                left[start : start + tile, :], weight[side], preferred_element_type=jnp.float32
            )
            mixed = mixed + packed[PBIAS : PBIAS + 1, ats[side]]
            mixed = mixed + frames[start : start + tile, ats[side]].astype(jnp.float32)
            result[side, start : start + tile, :] = mixed.astype(jnp.bfloat16)
            part = pltpu.make_async_copy(
                result.at[side, start : start + tile],
                out.at[start : start + tile, ats[side]],
                sems.at[len(copies) + len(parts)],
            )
            part.start()
            parts.append(part)
    for part in parts:
        part.wait()


def project(packed, signal, whole, places, pieces, spots, acts):
    length, width = signal.shape
    return pl.pallas_call(
        functools.partial(project_body, places, spots),
        in_specs=[VMEM] + [ANY] * (2 + len(pieces) + len(acts)),
        out_specs=ANY,
        out_shape=jax.ShapeDtypeStruct((length, width), jnp.bfloat16),
        scratch_shapes=[
            pltpu.VMEM((2, width, width // 2), jnp.bfloat16),
            pltpu.VMEM((length, width), jnp.bfloat16),
            pltpu.VMEM((length, width), jnp.bfloat16),
            pltpu.VMEM((2, length, width // 2), jnp.bfloat16),
            pltpu.SemaphoreType.DMA((sum(map(len, places)) + 3 + len(acts) + 2 * (length // 256),)),
        ],
        compiler_params=params(),
        cost_estimate=FREE,
        name="project_and_residual",
    )(packed, signal, whole, *pieces, *acts)


def across(array, axis, bits):
    count = lax.axis_size(axis)
    return lax.ppermute(array, axis, [(i, i ^ bits) for i in range(count)])


def after(array, *others):
    return lax.optimization_barrier((array, *others))[0]


def on_the_plane(
    signal, norm_gain, norm_bias, expand_weight, expand_bias, depth_kernel,
    batch_scale, batch_shift, project_weight, project_bias,
):
    width = signal.shape[2]
    own = signal[0]
    e_own, p_own, both = cut(expand_weight, project_weight, 4)
    beside = across(own, "seq", 1)
    facing = across(after(own, e_own), "seq", 2)
    e_far, e_near = across(e_own, "dp", 6), across(e_own, "dp", 2)
    y_own = across(both, "dp", 1)
    done = (e_far,  y_own)

    e_middle = across(after(e_own, *done), "dp", 4)
    p_near = across(after(p_own, *done), "dp", 2)
    ey_near, ey_far = across(after(e_near, *done), "dp", 1), across(after(e_far, *done), "dp", 1)
    packed = (
        jnp.concatenate(
            [after(norm_gain, *done), norm_bias, expand_bias, batch_scale, batch_shift, project_bias]
        )
        .reshape(7, width)
        .astype(jnp.float32)
    )
    normed = norm(packed, own)
    beside = norm(packed, beside)
    edges = jnp.concatenate([normed[:EDGE], normed[-EDGE:]], axis=0)
    done = (facing, e_middle, p_near, ey_near, ey_far, beside, edges)

    ey_middle = across(after(e_middle, *done), "dp", 1)
    p_far = across(after(p_own, *done), "dp", 6)
    edges = across(after(edges, *done), "seq", 3)
    py_near = across(after(p_near, *done), "dp", 1)
    normed_facing = norm(packed, after(facing, *done))
    diagonal = across(normed_facing, "seq", 1)
    e_shards = [e_own, e_near, e_middle, e_far, y_own, ey_near, ey_middle, ey_far]
    weight = gather([(2 * (k % 4) + k // 4, 0) for k in range(8)], e_shards)
    done = (ey_middle, edges, diagonal)

    run = functools.partial(conv, packed=packed, kernel=depth_kernel, weight=weight)
    part_facing = run(
        1, 0, 2, block=after(normed_facing, *done), sibling=edges, outer=beside
    )
    act_facing = [across(part, "seq", 2) for part in part_facing]
    p_middle = across(after(p_own, ey_middle, edges), "dp", 4)
    py_far = across(after(p_far, part_facing[0]), "dp", 1)
    done = (part_facing[0], p_far, py_near)

    [part_diagonal] = run(
        1, 1, 1, block=after(diagonal, *done), sibling=normed_facing, outer=normed
    )
    act_diagonal = across(part_diagonal, "seq", 3)
    [part_beside] = run(
        0, 1, 1, block=after(beside, part_diagonal), sibling=normed, outer=normed_facing
    )
    act_beside = across(part_beside, "seq", 1)
    [part_own] = run(
        0, 0, 1, block=after(normed, part_beside, py_far, *act_facing), sibling=beside, outer=diagonal
    )
    py_middle = across(after(p_middle, part_own), "dp", 1)
    columns = e_own.shape[1]
    early = gather([(None, 0), (None, columns)], [after(p_near, ey_middle), y_own])
    early_other = across(early, "seq", 1)
    late = [py_near, p_far, py_far, p_middle, py_middle]
    done = (part_own, act_diagonal, early_other)
    swapped = [across(after(shard, *done), "seq", 1) for shard in late]
    rows = e_own.shape[0]
    places = [
        [((1 + len(late)) * side, rows * k, bits) for k, bits in enumerate([2, 1])]
        + [((1 + len(late)) * side + 1 + k, 0, bits) for k, bits in enumerate([3, 6, 7, 4, 5])]
        for side in range(2)
    ]
    acts = [part_own, act_beside, act_diagonal, *act_facing]
    tall = own.shape[0] // len(act_facing)
    spots = [(0, 0), (1, 0), (3, 0)] + [(2, tall * k) for k in range(len(act_facing))]
    return project(packed, own, project_weight, places, [early, *late, early_other, *swapped], spots, acts)[None]


def extended(block, sides, width):
    for axis, dim in sides:
        count = lax.axis_size(axis)
        forward = [(i, i + 1) for i in range(count - 1)]
        backward = [(target, source) for source, target in forward]
        low = lax.ppermute(
            lax.slice_in_dim(block, block.shape[dim] - width, None, axis=dim), axis, forward
        )
        high = lax.ppermute(lax.slice_in_dim(block, 0, width, axis=dim), axis, backward)
        block = jnp.concatenate([low, block, high], axis=dim)
    return block


def fold_rows(left_side, blocks):
    return jnp.dot(left_side, blocks, preferred_element_type=jnp.float32)


def gathered(
    signal, norm_gain, norm_bias, expand_weight, expand_bias, depth_kernel,
    batch_scale, batch_shift, project_weight, project_bias,
):
    length = signal.shape[1]
    width = signal.shape[2]
    values = signal[0].astype(jnp.float32)
    average = jnp.mean(values, axis=-1, keepdims=True)
    centred = values - average
    spread = jnp.mean(centred * centred, axis=-1, keepdims=True)
    normed = (
        centred * lax.rsqrt(spread + 1e-05) * norm_gain.astype(jnp.float32)
        + norm_bias.astype(jnp.float32)
    ).astype(jnp.bfloat16)
    hidden = fold_rows(normed, lax.all_gather(expand_weight, "dp", axis=0, tiled=True))
    hidden = hidden + expand_bias.astype(jnp.float32)
    gated = (hidden[:, :width] * jax.nn.sigmoid(hidden[:, width:])).astype(jnp.bfloat16)
    halo_width = (depth_kernel.shape[0] - 1) // 2
    padded = extended(gated[None], (("seq", 1),), halo_width)[0].astype(jnp.float32)
    kernel = depth_kernel.astype(jnp.float32)
    depth = jnp.zeros((length, width), jnp.float32)
    for tap in range(depth_kernel.shape[0]):
        depth = depth + kernel[tap][None, :] * padded[tap : tap + length]
    scaled = depth * batch_scale.astype(jnp.float32) + batch_shift.astype(jnp.float32)
    activated = (scaled * jax.nn.sigmoid(scaled)).astype(jnp.bfloat16)
    mixed = fold_rows(activated, lax.all_gather(project_weight, "dp", axis=0, tiled=True))
    outcome = values + mixed + project_bias.astype(jnp.float32)
    return outcome.astype(jnp.bfloat16)[None]


def solution(mesh):
    local = on_the_plane if (mesh.shape["dp"], mesh.shape["seq"]) == (8, 4) else gathered
    in_specs = (
        P("dp", "seq", None),
        P(),
        P(),
        P("dp", None),
        P(),
        P(),
        P(),
        P(),
        P("dp", None),
        P(),
    )
    out_specs = P("dp", "seq", None)
    return jax.shard_map(local, mesh=mesh, in_specs=in_specs, out_specs=out_specs, check_vma=False)
```
